512 devices in a mesh: seq: 16 (over y, core), dp: 32 (over z, x).
Axes of the slice: x: 4, y: 8, z: 8, core: 2. Of those that a mesh axis runs over, the one named last changes fastest.
Arguments:
- queries: bfloat16 [32, 2048, 4096], P('dp', 'seq'), may hold values from -22 to 22
- key_vectors: bfloat16 [32, 2048, 512], P('dp', 'seq'), may hold values from -15 to 15
- value_vectors: bfloat16 [32, 2048, 512], P('dp', 'seq'), may hold values from -6 to 6
- forward_out: bfloat16 [32, 2048, 4096], P('dp', 'seq'), may hold values from -6 to 6
- out_grad: bfloat16 [32, 2048, 4096], P('dp', 'seq'), may hold values from -6 to 6
- segment_number: int32 [32, 2048], P('dp'), may hold values from 0 to 31, never falling along the last dimension, each value on 1 to 128 neighbouring positions
Outputs:
- query_grad: bfloat16 [32, 2048, 4096], P('dp', 'seq')
- key_grad: bfloat16 [32, 2048, 512], P('dp', 'seq')
- value_grad: bfloat16 [32, 2048, 512], P('dp', 'seq')
- bias_grad: float32 [5120], replicated
The draws below stay inside these ranges and needn't reach their ends.
Inputs may be any that keep to these rules, and one draw needn't show every extreme that they name: `segment_number`: within each microbatch the rollout numbers never fall, all of 0 to 31 occur, each rollout holds 1 to 128 positions and one holds exactly 128.
All inputs are finite; a program needn't handle non-finite values.
Results may differ from the reference program's by a relative error of at most 0.0055.
Values may be sent and summed in bfloat16 or wider, within the bound.
No kernel may reach another device: no remote copies, remote signals or barrier semaphores. Data moves between devices by JAX's collectives and lax.ppermute only.
A program may use at most 64 MiB of HBM per device.

```python
import math
import jax
import jax.numpy as jnp
import numpy as np
from jax import lax

HQ = 32
KVH = 4
HD = 128
S_DEV = 128
SEQ_LEN = 2048
SEGS = 32
MB = 32


def drawn_pair(key):
    streams = jax.random.split(key, 2)
    group_size = HQ // KVH
    key_rows = jax.random.truncated_normal(streams[0], -3.0, 3.0, (MB, SEQ_LEN, KVH, HD), jnp.float32)
    query_rows = jax.random.truncated_normal(streams[1], -3.0, 3.0, (MB, SEQ_LEN, KVH, group_size, HD), jnp.float32)
    return (query_rows.reshape(MB, SEQ_LEN, HQ * HD), key_rows.reshape(MB, SEQ_LEN, KVH * HD))


def draw_queries(key, part):
    return drawn_pair(key)[0].astype(jnp.bfloat16)


def draw_key_vectors(key, part):
    return drawn_pair(key)[1].astype(jnp.bfloat16)


def level_of(key, shape, pieces, smallest, top_value):
    def one(dim, blocks):
        steps = jax.random.uniform(jax.random.fold_in(jax.random.fold_in(key, 6), dim), (blocks,), jnp.float32, smallest / len(pieces), top_value / len(pieces))
        return jnp.repeat(jnp.exp(steps), shape[dim] // blocks).reshape((-1,) + (1,) * (len(shape) - dim - 1))

    gain = one(*pieces[0])
    for cut in pieces[1:]:
        gain = gain * one(*cut)
    return gain


def profile(count, total, most, lean):
    weights = [(1 << 20) // math.isqrt(grade ** lean) + 1 for grade in range(2, count + 1)]
    spare, holding = total - most - (count - 1), [1] * (count - 1)
    while spare > 0:
        free = [i for i in range(count - 1) if holding[i] < most]
        pool, budget = sum([weights[i] for i in free]), spare
        for i in free:
            addition = min(most - holding[i], max(1, budget * weights[i] // pool), spare)
            holding[i] = holding[i] + addition
            spare = spare - addition
    return np.array([most] + holding)


def uneven_parts(stream_key, count, total, bound, skew):
    if count == 2:
        one = jax.random.randint(stream_key, (), max(1, total - bound), min(bound, total - 1) + 1)
        return jnp.stack([one, total - one])
    tallies = jnp.asarray(profile(count, total, bound, skew), jnp.int32)
    pairs = (count - 1) // 2
    source_of, taker = tallies[1:1 + 2 * pairs:2], tallies[2:2 + 2 * pairs:2]
    slack = jnp.minimum(source_of - 1, bound - taker)
    moved = jax.random.randint(jax.random.fold_in(stream_key, 1), (pairs,), 0, 1 << 20) % (slack + 1)
    tallies = tallies.at[1:1 + 2 * pairs:2].set(source_of - moved).at[2:2 + 2 * pairs:2].set(taker + moved)
    return tallies[jax.random.permutation(jax.random.fold_in(stream_key, 2), count)]


def noise(stream_key, shape, scale, limit, cuts=(), dtype=jnp.bfloat16):
    result = jax.random.normal(stream_key, shape, jnp.float32) * scale
    if len(cuts) > 0:
        result = level_of(stream_key, shape, cuts, -0.22, 0.18) * result
    return jnp.clip(result, min=-limit, max=limit).astype(dtype)


def setup_inputs(seed: int = 0) -> dict:
    splits = jax.random.split(jax.random.key(seed), 7)
    queries = draw_queries(jax.random.fold_in(splits[6], 71), 0)
    key_vectors = draw_key_vectors(jax.random.fold_in(splits[6], 71), 0)
    value_vectors = noise(splits[2], (MB, SEQ_LEN, KVH * HD), 1.0, 6.0, ((0, 32), (1, 16)))
    forward_out = noise(splits[3], (MB, SEQ_LEN, HQ * HD), 1.0, 6.0, ((0, 32), (1, 16)))
    out_grad = noise(splits[4], (MB, SEQ_LEN, HQ * HD), 1.0, 6.0, ((0, 32), (1, 16)))
    segment_number = jax.vmap(lambda own: jnp.searchsorted(jnp.cumsum(uneven_parts(own, SEGS, SEQ_LEN, S_DEV, 2)), jnp.arange(SEQ_LEN), side="right"))(jax.random.split(splits[5], MB)).reshape((MB, SEQ_LEN)).astype(jnp.int32)
    return dict(queries=queries, key_vectors=key_vectors, value_vectors=value_vectors, forward_out=forward_out, out_grad=out_grad, segment_number=segment_number)


def group_backward(members):
    query_group, key_group, value_group, output_group, grad_group, segment_row = members
    block_rows = min(512, SEQ_LEN)
    score_scale = 1.0 / math.sqrt(HD)
    row_delta = lax.optimization_barrier(jnp.sum(grad_group.astype(jnp.float32) * output_group.astype(jnp.float32), axis=2))
    key_float = key_group.astype(jnp.float32)
    value_float = value_group.astype(jnp.float32)
    key_total = jnp.zeros((SEQ_LEN, HD), jnp.float32)
    value_total = jnp.zeros((SEQ_LEN, HD), jnp.float32)
    query_pieces = []
    for row_start in range(0, SEQ_LEN, block_rows):
        row_end = row_start + block_rows
        query_block = query_group[row_start:row_end].astype(jnp.float32)
        grad_block = grad_group[row_start:row_end].astype(jnp.float32)
        key_prefix = key_float[:row_end]
        value_prefix = value_float[:row_end]
        scores = jnp.einsum('ird,jd->rij', query_block, key_prefix) * score_scale
        key_positions = jnp.arange(row_end)
        row_positions = row_start + jnp.arange(block_rows)
        allowed = (segment_row[None, :row_end] == segment_row[row_start:row_end, None]) & (key_positions[None, :] <= row_positions[:, None])
        masked = jnp.where(allowed[None], scores, -jnp.inf)
        row_peak = lax.optimization_barrier(jnp.max(masked, axis=2, keepdims=True))
        log_total = row_peak + jnp.log(lax.optimization_barrier(jnp.sum(jnp.exp(masked - row_peak), axis=2, keepdims=True)))
        weights = jnp.exp(masked - log_total)
        weights_low = lax.optimization_barrier(weights.astype(jnp.bfloat16)).astype(jnp.float32)
        value_total = value_total.at[:row_end].add(jnp.einsum('rij,ird->jd', weights_low, grad_block))
        weight_grad = jnp.einsum('ird,jd->rij', grad_block, value_prefix)
        score_grad = weights * (weight_grad - jnp.transpose(row_delta[row_start:row_end])[:, :, None])
        score_low = lax.optimization_barrier(score_grad.astype(jnp.bfloat16)).astype(jnp.float32)
        query_pieces.append((jnp.einsum('rij,jd->ird', score_low, key_prefix) * score_scale).astype(jnp.bfloat16))
        key_total = key_total.at[:row_end].add(jnp.einsum('rij,ird->jd', score_low, query_block))
    return (jnp.concatenate(query_pieces, axis=0), key_total * score_scale, value_total)

def reference(queries, key_vectors, value_vectors, forward_out, out_grad, segment_number):
    group_size = HQ // KVH

    def heads_first(tensor):
        return tensor.reshape(MB, SEQ_LEN, KVH, group_size, HD).transpose(0, 2, 1, 3, 4).reshape(MB * KVH, SEQ_LEN, group_size, HD)

    def shared_first(tensor):
        return tensor.reshape(MB, SEQ_LEN, KVH, HD).transpose(0, 2, 1, 3).reshape(MB * KVH, SEQ_LEN, HD)
    segments = jnp.repeat(segment_number, KVH, axis=0)
    query_heads, key_heads, value_heads = lax.map(group_backward, (heads_first(queries), shared_first(key_vectors), shared_first(value_vectors), heads_first(forward_out), heads_first(out_grad), segments))
    query_grad = query_heads.reshape(MB, KVH, SEQ_LEN, group_size, HD).transpose(0, 2, 1, 3, 4).reshape(MB, SEQ_LEN, HQ * HD)
    key_grad = key_heads.reshape(MB, KVH, SEQ_LEN, HD).transpose(0, 2, 1, 3).reshape(MB, SEQ_LEN, KVH * HD).astype(jnp.bfloat16)
    value_grad = value_heads.reshape(MB, KVH, SEQ_LEN, HD).transpose(0, 2, 1, 3).reshape(MB, SEQ_LEN, KVH * HD).astype(jnp.bfloat16)
    bias_grad = jnp.concatenate([lax.optimization_barrier(jnp.sum(query_grad.astype(jnp.float32), axis=(0, 1))), lax.optimization_barrier(jnp.sum(key_grad.astype(jnp.float32), axis=(0, 1))), lax.optimization_barrier(jnp.sum(value_grad.astype(jnp.float32), axis=(0, 1)))])
    return (query_grad, key_grad, value_grad, bias_grad)
```

```python
import functools
import math

import jax
import jax.numpy as jnp
from jax import lax
from jax.experimental import pallas as pl
from jax.experimental.pallas import tpu as pltpu
from jax.sharding import PartitionSpec as P

HD = 128
ROWS = 128
GROUP = 8
NEG = -1e30
SCALE = 1.0 / math.sqrt(HD)
SCALE2 = SCALE * math.log2(math.e)
TN = (((1,), (1,)), ((), ()))
NN = (((1,), (0,)), ((), ()))


def dot(a, b, dims=NN):
    return lax.dot_general(a, b, dims, preferred_element_type=jnp.float32)


def attention_kernel(
    me_ref, seg_ref, q_ref, o_ref, do_ref, kc_ref, vc_ref, kp_ref, vp_ref,
    dq_ref, own_ref, back_ref, sums_ref,
    mask_ref, w_ref, ds_ref,
):
    group = pl.program_id(0)
    shared = pl.num_programs(0)

    @pl.when(group == 0)
    def _():
        me = me_ref[0]
        before = jnp.maximum(me - 1, 0)
        seg_own = jnp.broadcast_to(seg_ref[pl.ds(me, 1), :], (ROWS, ROWS))
        seg_before = jnp.broadcast_to(seg_ref[pl.ds(before, 1), :], (ROWS, ROWS))
        key = lax.broadcasted_iota(jnp.int32, (ROWS, ROWS), 0)
        row = lax.broadcasted_iota(jnp.int32, (ROWS, ROWS), 1)
        own_col = jnp.sum(jnp.where(key == row, seg_own, 0), axis=1, keepdims=True)
        before_col = jnp.sum(jnp.where(key == row, seg_before, 0), axis=1, keepdims=True)
        mask_ref[0:ROWS, :] = jnp.where((before_col == seg_own) & (me > 0), 0.0, NEG)
        mask_ref[ROWS : 2 * ROWS, :] = jnp.where((own_col == seg_own) & (key <= row), 0.0, NEG)

    keys = jnp.concatenate([kp_ref[...], kc_ref[...]], axis=0)
    values = jnp.concatenate([vp_ref[...], vc_ref[...]], axis=0)
    keys_t = keys.T
    mask = mask_ref[...]
    query_sums = []
    for head in range(GROUP):
        at = slice(head * HD, (head + 1) * HD)
        q = q_ref[:, at]
        do = do_ref[:, at]
        products = do.astype(jnp.float32) * o_ref[:, at].astype(jnp.float32)
        delta = jnp.sum(products.T, axis=0, keepdims=True)
        scores = dot(keys, q, TN) * SCALE2 + mask
        peak = jnp.max(scores, axis=0, keepdims=True)
        powers = jnp.exp2(scores - peak)
        total = jnp.sum(powers, axis=0, keepdims=True)
        weights = powers * (1.0 / total)
        w_ref[:, at] = weights.astype(jnp.bfloat16)
        score_grad = weights * (dot(values, do, TN) - delta)
        score_low = score_grad.astype(jnp.bfloat16)
        ds_ref[:, at] = score_low
        dq = (dot(keys_t, score_low).T * SCALE).astype(jnp.bfloat16)
        dq_ref[:, at] = dq
        query_sums.append(jnp.sum(dq.astype(jnp.float32), axis=0, keepdims=True))
    sums_ref[pl.ds(group * GROUP, GROUP), :] = jnp.concatenate(query_sums, axis=0)

    def stacked(ref):
        return jnp.concatenate([ref[:, h * HD : (h + 1) * HD] for h in range(GROUP)], axis=0)

    key_part = dot(ds_ref[...], stacked(q_ref)) * SCALE
    value_part = dot(w_ref[...], stacked(do_ref))
    back_ref[0] = key_part[:ROWS]
    back_ref[1] = value_part[:ROWS]
    own_ref[0] = key_part[ROWS:]
    own_ref[1] = value_part[ROWS:]
    base = shared * GROUP
    sums_ref[pl.ds(base + group, 1), :] = jnp.sum(key_part, axis=0, keepdims=True)
    sums_ref[pl.ds(base + shared + group, 1), :] = jnp.sum(value_part, axis=0, keepdims=True)


def attention(me, segments, queries, forward_out, out_grad, own, before):
    shared = own.shape[1] // (2 * HD)
    wide = pl.BlockSpec((ROWS, GROUP * HD), lambda g: (0, g))
    key_spec = pl.BlockSpec((ROWS, HD), lambda g: (0, g))
    value_spec = pl.BlockSpec((ROWS, HD), lambda g: (0, shared + g))
    part_spec = pl.BlockSpec((2, ROWS, HD), lambda g: (0, 0, g))
    sum_rows = shared * GROUP + 2 * shared
    return pl.pallas_call(
        attention_kernel,
        grid=(shared,),
        in_specs=[
            pl.BlockSpec(memory_space=pltpu.SMEM),
            pl.BlockSpec(segments.shape, lambda g: (0, 0)),
            wide, wide, wide,
            key_spec, value_spec, key_spec, value_spec,
        ],
        out_specs=[wide, part_spec, part_spec, pl.BlockSpec((sum_rows, HD), lambda g: (0, 0))],
        out_shape=[
            jax.ShapeDtypeStruct(queries.shape, jnp.bfloat16),
            jax.ShapeDtypeStruct((2, ROWS, shared * HD), jnp.float32),
            jax.ShapeDtypeStruct((2, ROWS, shared * HD), jnp.float32),
            jax.ShapeDtypeStruct((sum_rows, HD), jnp.float32),
        ],
        scratch_shapes=[
            pltpu.VMEM((2 * ROWS, ROWS), jnp.float32),
            pltpu.VMEM((2 * ROWS, GROUP * HD), jnp.bfloat16),
            pltpu.VMEM((2 * ROWS, GROUP * HD), jnp.bfloat16),
        ],
        compiler_params=pltpu.CompilerParams(vmem_limit_bytes=32 * 1024 * 1024),
        cost_estimate=pl.CostEstimate(
            flops=10 * 2 * ROWS * ROWS * HD * shared * GROUP,
            bytes_accessed=5 * 1024 * 1024,
            transcendentals=2 * ROWS * ROWS * shared * GROUP,
        ),
    )(me, segments, queries, forward_out, out_grad, own, own, before, before)


def cosets(size, masks):
    span = [0]
    for m in masks:
        span = span + [a ^ m for a in span]
    groups, seen = [], set()
    for i in range(size):
        if i not in seen:
            group = sorted(i ^ a for a in span)
            groups.append(group)
            seen |= set(group)
    return groups


def group_sum(x, axis, masks):
    groups = cosets(lax.axis_size(axis), masks)
    count = len(groups[0])
    if count == 2:
        parts = lax.all_gather(x, axis, axis_index_groups=groups)
    else:
        copies = jnp.broadcast_to(x[None], (count,) + x.shape)
        parts = lax.all_to_all(
            copies, axis, split_axis=0, concat_axis=0, tiled=True, axis_index_groups=groups
        )
    return jnp.sum(parts, axis=0)


def global_sum(x):
    for axis, masks in (("seq", [1]), ("seq", [2, 4, 8]), ("dp", [1, 2]), ("dp", [4, 8, 16])):
        x = group_sum(x, axis, [m for m in masks if m < lax.axis_size(axis)])
    return x


def per_device(queries, key_vectors, value_vectors, forward_out, out_grad, segment_number):
    ways = lax.axis_size("seq")
    me = lax.axis_index("seq")
    own = jnp.concatenate([key_vectors[0], value_vectors[0]], axis=1)
    before = lax.ppermute(own, "seq", [(i, i + 1) for i in range(ways - 1)])
    segments = segment_number.reshape(ways, ROWS)
    query_grad, kept, back, sums = attention(
        me.astype(jnp.int32).reshape(1), segments, queries[0], forward_out[0], out_grad[0], own, before
    )
    returned = lax.ppermute(back, "seq", [(i + 1, i) for i in range(ways - 1)])
    both = (kept + returned).astype(jnp.bfloat16)
    bias_grad = global_sum(sums).reshape(-1)
    return (query_grad[None], both[0][None], both[1][None], bias_grad)


def solution(mesh):
    rows = P("dp", "seq", None)
    return jax.shard_map(
        per_device,
        mesh=mesh,
        in_specs=(rows, rows, rows, rows, rows, P("dp", None)),
        out_specs=(rows, rows, rows, P()),
        check_vma=False,
    )
```

```python
import math

import jax
import jax.numpy as jnp
from jax import lax
from jax.experimental import pallas as pl
from jax.experimental.pallas import tpu as pltpu
from jax.sharding import PartitionSpec as P

HD = 128
ROWS = 128
GROUP = 8
NEG = -1e30
SCALE = 1.0 / math.sqrt(HD)
SCALE2 = SCALE * math.log2(math.e)
NT = (((1,), (1,)), ((), ()))
NN = (((1,), (0,)), ((), ()))


def dot(a, b, dims=NN):
    return lax.dot_general(a, b, dims, preferred_element_type=jnp.float32)


def column(row):
    key = lax.broadcasted_iota(jnp.int32, (ROWS, ROWS), 0)
    at = lax.broadcasted_iota(jnp.int32, (ROWS, ROWS), 1)
    return jnp.sum(jnp.where(key == at, jnp.broadcast_to(row, (ROWS, ROWS)), 0), axis=1, keepdims=True)


def heads(width=HD):
    return [slice(h * width, (h + 1) * width) for h in range(GROUP)]


def own_kernel(
    me_ref, seg_ref, q_ref, o_ref, do_ref, k_ref, v_ref,
    power_ref, slope_ref, qs_ref, dos_ref, ks_ref, stat_ref, before_mask_ref, mask_ref,
):
    group = pl.program_id(0)

    @pl.when(group == 0)
    def _():
        me = me_ref[0]
        seg = seg_ref[pl.ds(me, 1), :]
        seg_before = seg_ref[pl.ds(jnp.maximum(me - 1, 0), 1), :]
        key = lax.broadcasted_iota(jnp.int32, (ROWS, ROWS), 0)
        row = lax.broadcasted_iota(jnp.int32, (ROWS, ROWS), 1)
        mask_ref[...] = jnp.where((column(seg) == seg) & (key <= row), 0.0, NEG)
        before_mask_ref[...] = jnp.where((column(seg_before) == seg) & (me > 0), 0.0, NEG)

    mask = mask_ref[...]
    q_all = jnp.concatenate([q_ref[:, at] for at in heads()], axis=0)
    do_all = jnp.concatenate([do_ref[:, at] for at in heads()], axis=0)
    qs_ref[group] = q_all
    dos_ref[group] = do_all
    ks_ref[group] = k_ref[...]
    scores_all = dot(k_ref[...], q_all, NT)
    grads_all = dot(v_ref[...], do_all, NT)
    for at in heads():
        products = do_ref[:, at].astype(jnp.float32) * o_ref[:, at].astype(jnp.float32)
        delta = jnp.sum(products.T, axis=0, keepdims=True)
        scores = scores_all[:, at] * SCALE2 + mask
        peak = jnp.max(scores, axis=0, keepdims=True)
        powers = jnp.exp2(scores - peak)
        power_ref[group, :, at] = powers
        slope_ref[group, :, at] = powers * (grads_all[:, at] - delta)
        stat_ref[group, 0:1, at] = peak
        stat_ref[group, 1:2, at] = jnp.sum(powers, axis=0, keepdims=True)
        stat_ref[group, 2:3, at] = delta


def whole_kernel(
    power_ref, slope_ref, qs_ref, dos_ref, ks_ref, stat_ref, mask_ref, k_before_ref, v_before_ref,
    dq_ref, kept_ref, back_ref, sums_ref,
    w_ref, ds_ref, dq_buf, sems,
):
    shared = power_ref.shape[0]
    mask = mask_ref[...]
    copies = []
    for group in range(shared):
        k_at = slice(group * HD, (group + 1) * HD)
        k_before = k_before_ref[:, k_at]
        v_before = v_before_ref[:, k_at]
        keys_t = jnp.concatenate([k_before, ks_ref[group]], axis=0).T
        q_all = qs_ref[group]
        do_all = dos_ref[group]
        scores_all = dot(k_before, q_all, NT)
        grads_all = dot(v_before, do_all, NT)
        for at in heads():
            peak_own = stat_ref[group, 0:1, at]
            scores = scores_all[:, at] * SCALE2 + mask
            peak = jnp.maximum(jnp.max(scores, axis=0, keepdims=True), peak_own)
            powers = jnp.exp2(scores - peak)
            fade = jnp.exp2(peak_own - peak)
            total = jnp.sum(powers, axis=0, keepdims=True) + stat_ref[group, 1:2, at] * fade
            share = 1.0 / total
            weights = powers * share
            share_own = fade * share
            w_ref[group, 0:ROWS, at] = weights.astype(jnp.bfloat16)
            w_ref[group, ROWS:, at] = (power_ref[group, :, at] * share_own).astype(jnp.bfloat16)
            ds_ref[group, 0:ROWS, at] = (weights * (grads_all[:, at] - stat_ref[group, 2:3, at])).astype(jnp.bfloat16)
            ds_ref[group, ROWS:, at] = (slope_ref[group, :, at] * share_own).astype(jnp.bfloat16)
        dq_t = (dot(keys_t, ds_ref[group]) * SCALE).astype(jnp.bfloat16)
        for head, at in enumerate(heads()):
            dq = dq_t[:, at].T
            dq_buf[group, :, at] = dq
            row = group * GROUP + head
            sums_ref[row : row + 1, :] = jnp.sum(dq.astype(jnp.float32), axis=0, keepdims=True)
        copies.append(
            pltpu.make_async_copy(
                dq_buf.at[group], dq_ref.at[:, pl.ds(group * GROUP * HD, GROUP * HD)], sems.at[group]
            )
        )
        copies[-1].start()
        key_part = dot(ds_ref[group], q_all) * SCALE
        value_part = dot(w_ref[group], do_all)
        back_ref[0, :, k_at] = key_part[:ROWS]
        back_ref[1, :, k_at] = value_part[:ROWS]
        kept_ref[0, :, k_at] = key_part[ROWS:]
        kept_ref[1, :, k_at] = value_part[ROWS:]
        base = shared * GROUP + group
        sums_ref[base : base + 1, :] = jnp.sum(key_part, axis=0, keepdims=True)
        sums_ref[base + shared : base + shared + 1, :] = jnp.sum(value_part, axis=0, keepdims=True)
    for copy in copies:
        copy.wait()


VMEM = pl.BlockSpec(memory_space=pltpu.VMEM)
SMEM = pl.BlockSpec(memory_space=pltpu.SMEM)


def own_part(me, segments, queries, forward_out, out_grad, keys, values):
    shared = keys.shape[1] // HD
    wide = pl.BlockSpec((ROWS, GROUP * HD), lambda g: (0, g))
    narrow = pl.BlockSpec((ROWS, HD), lambda g: (0, g))
    hbm = [pltpu.with_memory_space_constraint(x, pltpu.HBM) for x in (queries, forward_out, out_grad, keys, values)]
    terms = (shared, ROWS, GROUP * ROWS)
    stacked = (shared, GROUP * ROWS, HD)
    return pl.pallas_call(
        own_kernel,
        grid=(shared,),
        in_specs=[SMEM, pl.BlockSpec(segments.shape, lambda g: (0, 0)), wide, wide, wide, narrow, narrow],
        out_specs=[VMEM] * 7,
        out_shape=[
            pltpu.VMEM(terms, jnp.float32),
            pltpu.VMEM(terms, jnp.float32),
            pltpu.VMEM(stacked, jnp.bfloat16),
            pltpu.VMEM(stacked, jnp.bfloat16),
            pltpu.VMEM((shared, ROWS, HD), jnp.bfloat16),
            pltpu.VMEM((shared, 8, GROUP * ROWS), jnp.float32),
            pltpu.VMEM((ROWS, ROWS), jnp.float32),
        ],
        scratch_shapes=[pltpu.VMEM((ROWS, ROWS), jnp.float32)],
        compiler_params=pltpu.CompilerParams(vmem_limit_bytes=24 * 1024 * 1024),
        cost_estimate=pl.CostEstimate(
            flops=4 * 2 * ROWS * ROWS * HD * shared * GROUP,
            bytes_accessed=4 * 1024 * 1024,
            transcendentals=ROWS * ROWS * shared * GROUP,
        ),
    )(me, pltpu.with_memory_space_constraint(segments, pltpu.HBM), *hbm)


def whole_part(terms, keys_before, values_before):
    shared = keys_before.shape[1] // HD
    sum_rows = shared * GROUP + 2 * shared
    pinned = [pltpu.with_memory_space_constraint(x, pltpu.VMEM) for x in (*terms, keys_before, values_before)]
    return pl.pallas_call(
        whole_kernel,
        in_specs=[VMEM] * 9,
        out_specs=[pl.BlockSpec(memory_space=pltpu.HBM), VMEM, VMEM, VMEM],
        out_shape=[
            jax.ShapeDtypeStruct((ROWS, shared * GROUP * HD), jnp.bfloat16),
            pltpu.VMEM((2, ROWS, shared * HD), jnp.float32),
            pltpu.VMEM((2, ROWS, shared * HD), jnp.float32),
            pltpu.VMEM((sum_rows, HD), jnp.float32),
        ],
        scratch_shapes=[
            pltpu.VMEM((shared, 2 * ROWS, GROUP * ROWS), jnp.bfloat16),
            pltpu.VMEM((shared, 2 * ROWS, GROUP * ROWS), jnp.bfloat16),
            pltpu.VMEM((shared, ROWS, GROUP * HD), jnp.bfloat16),
            pltpu.SemaphoreType.DMA((shared,)),
        ],
        compiler_params=pltpu.CompilerParams(vmem_limit_bytes=32 * 1024 * 1024),
        cost_estimate=pl.CostEstimate(
            flops=7 * 2 * ROWS * ROWS * HD * shared * GROUP,
            bytes_accessed=3 * 1024 * 1024,
            transcendentals=ROWS * ROWS * shared * GROUP,
        ),
    )(*pinned)


def group_sum(x, masks):
    span = [0]
    for m in masks:
        span = span + [a ^ m for a in span]
    groups, seen = [], set()
    for i in range(lax.axis_size("seq") * lax.axis_size("dp")):
        if i not in seen:
            groups.append(sorted(i ^ a for a in span))
            seen |= set(groups[-1])
    copies = jnp.broadcast_to(x[None], (len(span),) + x.shape)
    parts = lax.all_to_all(
        copies, ("seq", "dp"), split_axis=0, concat_axis=0, tiled=True, axis_index_groups=groups
    )
    return jnp.sum(parts, axis=0)


def bits(low, high):
    return [low << i for i in range((high // low).bit_length() - 1)]


def per_device(queries, key_vectors, value_vectors, forward_out, out_grad, segment_number):
    ways = lax.axis_size("seq")
    me = lax.axis_index("seq").astype(jnp.int32).reshape(1)
    onward = [(i, i + 1) for i in range(ways - 1)]
    keys_before = lax.ppermute(key_vectors[0], "seq", onward)
    values_before = lax.ppermute(value_vectors[0], "seq", onward)
    segments = segment_number.reshape(ways, ROWS)
    terms = own_part(
        me, segments, queries[0], forward_out[0], out_grad[0], key_vectors[0], value_vectors[0]
    )
    query_grad, kept, back, sums = whole_part(terms, keys_before, values_before)
    low = back.astype(jnp.bfloat16)
    returned = lax.ppermute(low, "seq", [(i + 1, i) for i in range(ways - 1)])
    places = lax.axis_size("dp")
    sums = group_sum(sums, bits(2 * places, ways * places))
    both = (kept + returned.astype(jnp.float32)).astype(jnp.bfloat16)
    sums = group_sum(sums, [places] + bits(1, 4))
    sums = group_sum(sums, bits(4, places))
    return (query_grad[None], both[0][None], both[1][None], sums.reshape(-1))


def solution(mesh):
    rows = P("dp", "seq", None)
    return jax.shard_map(
        per_device,
        mesh=mesh,
        in_specs=(rows, rows, rows, rows, rows, P("dp", None)),
        out_specs=(rows, rows, rows, P()),
        check_vma=False,
    )
```

```python
import math

import jax
import jax.numpy as jnp
from jax import lax
from jax.experimental import pallas as pl
from jax.experimental.pallas import tpu as pltpu
from jax.sharding import PartitionSpec as P

HD = 128
ROWS = 128
GROUP = 8
NEG = -1e30
SCALE = 1.0 / math.sqrt(HD)
SCALE2 = SCALE * math.log2(math.e)
NT = (((1,), (1,)), ((), ()))
NN = (((1,), (0,)), ((), ()))
TN = (((0,), (0,)), ((), ()))


VMEM = pl.BlockSpec(memory_space=pltpu.VMEM)
SMEM = pl.BlockSpec(memory_space=pltpu.SMEM)
HBM = pl.BlockSpec(memory_space=pltpu.HBM)


def dot(a, b, dims=NN):
    return lax.dot_general(a, b, dims, preferred_element_type=jnp.float32)


def column(row):
    key = lax.broadcasted_iota(jnp.int32, (ROWS, ROWS), 0)
    at = lax.broadcasted_iota(jnp.int32, (ROWS, ROWS), 1)
    return jnp.sum(jnp.where(key == at, jnp.broadcast_to(row, (ROWS, ROWS)), 0), axis=1, keepdims=True)


def heads(width=HD):
    return [slice(h * width, (h + 1) * width) for h in range(GROUP)]


def own_kernel(
    me_ref, seg_hbm, q_hbm, o_hbm, do_hbm, k_hbm, v_hbm,
    power_ref, slope_ref, qs_ref, dos_ref, keys_ref, stat_ref, before_mask_ref,
    seg_ref, q_ref, o_ref, do_ref, v_ref, sems,
):
    shared = power_ref.shape[0]
    first = [
        pltpu.make_async_copy(src, dst, sems.at[3 * shared + n])
        for n, (src, dst) in enumerate(((seg_hbm, seg_ref), (k_hbm, keys_ref), (v_hbm, v_ref)))
    ]
    for copy in first:
        copy.start()
    copies = []
    for group in range(shared):
        at = pl.ds(group * GROUP * HD, GROUP * HD)
        copies.append(
            [
                pltpu.make_async_copy(src.at[:, at], dst.at[:, at], sems.at[3 * group + n])
                for n, (src, dst) in enumerate(((q_hbm, q_ref), (do_hbm, do_ref), (o_hbm, o_ref)))
            ]
        )
        for copy in copies[-1]:
            copy.start()
    for copy in first:
        copy.wait()
    me = me_ref[0]
    seg = seg_ref[pl.ds(me, 1), :]
    seg_before = seg_ref[pl.ds(jnp.maximum(me - 1, 0), 1), :]
    key = lax.broadcasted_iota(jnp.int32, (ROWS, ROWS), 0)
    row = lax.broadcasted_iota(jnp.int32, (ROWS, ROWS), 1)
    mask = jnp.where((column(seg) == seg) & (key <= row), 0.0, NEG)
    before_mask_ref[...] = jnp.where((column(seg_before) == seg) & (me > 0), 0.0, NEG)
    for group in range(shared):
        for copy in copies[group]:
            copy.wait()
        cols = [slice((group * GROUP + h) * HD, (group * GROUP + h + 1) * HD) for h in range(GROUP)]
        q_all = jnp.concatenate([q_ref[:, c] for c in cols], axis=0)
        do_all = jnp.concatenate([do_ref[:, c] for c in cols], axis=0)
        qs_ref[group] = q_all
        dos_ref[group] = do_all
        mine = slice(group * HD, (group + 1) * HD)
        scores_all = dot(keys_ref[:, mine], q_all, NT)
        grads_all = dot(v_ref[:, mine], do_all, NT)
        for c, at in zip(cols, heads()):
            products = do_ref[:, c].astype(jnp.float32) * o_ref[:, c].astype(jnp.float32)
            delta = jnp.sum(products.T, axis=0, keepdims=True)
            scores = scores_all[:, at] * SCALE2 + mask
            peak = jnp.max(scores, axis=0, keepdims=True)
            powers = jnp.exp2(scores - peak)
            power_ref[group, :, at] = powers
            slope_ref[group, :, at] = powers * (grads_all[:, at] - delta)
            stat_ref[group, 0:1, at] = peak
            stat_ref[group, 1:2, at] = jnp.sum(powers, axis=0, keepdims=True)
            stat_ref[group, 2:3, at] = delta


def weight_kernel(
    power_ref, slope_ref, qs_ref, dos_ref, stat_ref, mask_ref, k_before_ref,
    weight_ref, ds_own_ref, kept_ref, back_ref, sums_ref,
    w_ref,
):
    shared = power_ref.shape[0]
    mask = mask_ref[...]
    for group in range(shared):
        mine = slice(group * HD, (group + 1) * HD)
        scores_all = dot(k_before_ref[:, mine], qs_ref[group], NT)
        for at in heads():
            peak_own = stat_ref[group, 0:1, at]
            scores = scores_all[:, at] * SCALE2 + mask
            peak = jnp.maximum(jnp.max(scores, axis=0, keepdims=True), peak_own)
            powers = jnp.exp2(scores - peak)
            fade = jnp.exp2(peak_own - peak)
            total = jnp.sum(powers, axis=0, keepdims=True) + stat_ref[group, 1:2, at] * fade
            share = 1.0 / total
            weights = powers * share
            share_own = fade * share
            weight_ref[group, :, at] = weights
            w_ref[group, 0:ROWS, at] = weights.astype(jnp.bfloat16)
            w_ref[group, ROWS:, at] = (power_ref[group, :, at] * share_own).astype(jnp.bfloat16)
            ds_own_ref[group, :, at] = (slope_ref[group, :, at] * share_own).astype(jnp.bfloat16)
        value_part = dot(w_ref[group], dos_ref[group])
        back_ref[:, mine] = value_part[:ROWS].astype(jnp.bfloat16)
        kept_ref[:, mine] = value_part[ROWS:]
        sums_ref[group : group + 1, :] = jnp.sum(value_part, axis=0, keepdims=True)


def score_kernel(
    weight_ref, ds_own_ref, qs_ref, dos_ref, stat_ref, keys_ref, k_before_ref, v_before_ref, value_back_ref, value_sums_ref,
    dq_ref, kept_ref, back_ref, sums_ref,
    ds_ref, dq_buf, sems,
):
    shared = weight_ref.shape[0]
    base = shared * GROUP
    back_ref[1] = value_back_ref[...]
    sums_ref[base + shared : base + 2 * shared, :] = value_sums_ref[0:shared, :]
    copies = []
    for group in range(shared):
        mine = slice(group * HD, (group + 1) * HD)
        keys = jnp.concatenate([k_before_ref[:, mine], keys_ref[:, mine]], axis=0)
        grads_all = dot(v_before_ref[:, mine], dos_ref[group], NT)
        ds_ref[group, ROWS:, :] = ds_own_ref[group]
        for at in heads():
            slope = weight_ref[group, :, at] * (grads_all[:, at] - stat_ref[group, 2:3, at])
            ds_ref[group, 0:ROWS, at] = slope.astype(jnp.bfloat16)
        for head, at in enumerate(heads()):
            dq = (dot(ds_ref[group, :, at], keys, TN) * SCALE).astype(jnp.bfloat16)
            dq_buf[group, :, at] = dq
            row = group * GROUP + head
            sums_ref[row : row + 1, :] = jnp.sum(dq.astype(jnp.float32), axis=0, keepdims=True)
        copies.append(
            pltpu.make_async_copy(
                dq_buf.at[group], dq_ref.at[:, pl.ds(group * GROUP * HD, GROUP * HD)], sems.at[group]
            )
        )
        copies[-1].start()
        key_part = dot(ds_ref[group], qs_ref[group]) * SCALE
        back_ref[0, :, mine] = key_part[:ROWS].astype(jnp.bfloat16)
        kept_ref[:, mine] = key_part[ROWS:]
        sums_ref[base + group : base + group + 1, :] = jnp.sum(key_part, axis=0, keepdims=True)
    for copy in copies:
        copy.wait()


def own_part(me, segments, queries, forward_out, out_grad, keys, values):
    shared = keys.shape[1] // HD
    hbm = [pltpu.with_memory_space_constraint(x, pltpu.HBM) for x in (segments, queries, forward_out, out_grad, keys, values)]
    terms = (shared, ROWS, GROUP * ROWS)
    stacked = (shared, GROUP * ROWS, HD)
    return pl.pallas_call(
        own_kernel,
        in_specs=[SMEM] + [HBM] * 6,
        out_specs=[VMEM] * 7,
        out_shape=[
            pltpu.VMEM(terms, jnp.float32),
            pltpu.VMEM(terms, jnp.float32),
            pltpu.VMEM(stacked, jnp.bfloat16),
            pltpu.VMEM(stacked, jnp.bfloat16),
            pltpu.VMEM(keys.shape, jnp.bfloat16),
            pltpu.VMEM((shared, 8, GROUP * ROWS), jnp.float32),
            pltpu.VMEM((ROWS, ROWS), jnp.float32),
        ],
        scratch_shapes=[
            pltpu.VMEM(segments.shape, jnp.int32),
            pltpu.VMEM(queries.shape, jnp.bfloat16),
            pltpu.VMEM(queries.shape, jnp.bfloat16),
            pltpu.VMEM(queries.shape, jnp.bfloat16),
            pltpu.VMEM(values.shape, jnp.bfloat16),
            pltpu.SemaphoreType.DMA((3 * shared + 3,)),
        ],
        compiler_params=pltpu.CompilerParams(vmem_limit_bytes=32 * 1024 * 1024),
        cost_estimate=pl.CostEstimate(
            flops=4 * 2 * ROWS * ROWS * HD * shared * GROUP,
            bytes_accessed=4 * 1024 * 1024,
            transcendentals=ROWS * ROWS * shared * GROUP,
        ),
    )(me, *hbm)


def pin(*arrays):
    return [pltpu.with_memory_space_constraint(x, pltpu.VMEM) for x in arrays]


def weight_part(terms, keys_before):
    power, slope, queries, grads, _, stats, mask = terms
    shared = power.shape[0]
    return pl.pallas_call(
        weight_kernel,
        in_specs=[VMEM] * 7,
        out_specs=[VMEM] * 5,
        out_shape=[
            pltpu.VMEM(power.shape, jnp.float32),
            pltpu.VMEM(power.shape, jnp.bfloat16),
            pltpu.VMEM(keys_before.shape, jnp.float32),
            pltpu.VMEM(keys_before.shape, jnp.bfloat16),
            pltpu.VMEM((8, HD), jnp.float32),
        ],
        scratch_shapes=[pltpu.VMEM((shared, 2 * ROWS, GROUP * ROWS), jnp.bfloat16)],
        compiler_params=pltpu.CompilerParams(vmem_limit_bytes=24 * 1024 * 1024),
        cost_estimate=pl.CostEstimate(
            flops=3 * 2 * ROWS * ROWS * HD * shared * GROUP,
            bytes_accessed=1024 * 1024,
            transcendentals=ROWS * ROWS * shared * GROUP,
        ),
    )(*pin(power, slope, queries, grads, stats, mask, keys_before))


def score_part(terms, weights, ds_own, keys_before, values_before, value_back, value_sums):
    _, _, queries, grads, keys, stats, _ = terms
    shared = weights.shape[0]
    return pl.pallas_call(
        score_kernel,
        in_specs=[VMEM] * 10,
        out_specs=[HBM, VMEM, VMEM, VMEM],
        out_shape=[
            jax.ShapeDtypeStruct((ROWS, shared * GROUP * HD), jnp.bfloat16),
            pltpu.VMEM(keys.shape, jnp.float32),
            pltpu.VMEM((2,) + keys.shape, jnp.bfloat16),
            pltpu.VMEM((shared * GROUP + 2 * shared, HD), jnp.float32),
        ],
        scratch_shapes=[
            pltpu.VMEM((shared, 2 * ROWS, GROUP * ROWS), jnp.bfloat16),
            pltpu.VMEM((shared, ROWS, GROUP * HD), jnp.bfloat16),
            pltpu.SemaphoreType.DMA((shared,)),
        ],
        compiler_params=pltpu.CompilerParams(vmem_limit_bytes=24 * 1024 * 1024),
        cost_estimate=pl.CostEstimate(
            flops=5 * 2 * ROWS * ROWS * HD * shared * GROUP,
            bytes_accessed=2 * 1024 * 1024,
            transcendentals=0,
        ),
    )(*pin(weights, ds_own, queries, grads, stats, keys, keys_before, values_before, value_back, value_sums))


def group_parts(x, masks):
    span = [0]
    for m in masks:
        span = span + [a ^ m for a in span]
    groups, seen = [], set()
    for i in range(lax.axis_size("seq") * lax.axis_size("dp")):
        if i not in seen:
            groups.append(sorted(i ^ a for a in span))
            seen |= set(groups[-1])
    copies = jnp.broadcast_to(x[None], (len(span),) + x.shape)
    return lax.all_to_all(
        copies, ("seq", "dp"), split_axis=0, concat_axis=0, tiled=True, axis_index_groups=groups
    )


def bits(low, high):
    return [low << i for i in range((high // low).bit_length() - 1)]


def closing_kernel(parts_ref, key_kept_ref, value_kept_ref, returned_ref, bias_ref, key_ref, value_ref):
    bias_ref[...] = jnp.sum(parts_ref[...], axis=0)
    key_ref[...] = (key_kept_ref[...] + returned_ref[0].astype(jnp.float32)).astype(jnp.bfloat16)
    value_ref[...] = (value_kept_ref[...] + returned_ref[1].astype(jnp.float32)).astype(jnp.bfloat16)


def closing(parts, key_kept, value_kept, returned):
    grad = jax.ShapeDtypeStruct(key_kept.shape, jnp.bfloat16)
    return pl.pallas_call(
        closing_kernel,
        in_specs=[VMEM] * 4,
        out_specs=[VMEM] * 3,
        out_shape=[jax.ShapeDtypeStruct(parts.shape[1:], jnp.float32), grad, grad],
    )(*pin(parts, key_kept, value_kept, returned))


def per_device(queries, key_vectors, value_vectors, forward_out, out_grad, segment_number):
    ways = lax.axis_size("seq")
    me = lax.axis_index("seq").astype(jnp.int32).reshape(1)
    onward = [(i, i + 1) for i in range(ways - 1)]
    keys_before = lax.ppermute(key_vectors[0], "seq", onward)
    values_before = lax.ppermute(value_vectors[0], "seq", onward)
    segments = segment_number.reshape(ways, ROWS)
    terms = own_part(
        me, segments, queries[0], forward_out[0], out_grad[0], key_vectors[0], value_vectors[0]
    )
    weights, ds_own, value_kept, value_back, value_sums = weight_part(terms, keys_before)
    query_grad, key_kept, back, sums = score_part(
        terms, weights, ds_own, keys_before, values_before, value_back, value_sums
    )
    returned = lax.ppermute(back, "seq", [(i + 1, i) for i in range(ways - 1)])
    places = lax.axis_size("dp")
    sums = jnp.sum(group_parts(sums, bits(2 * places, ways * places)), axis=0)
    sums = jnp.sum(group_parts(sums, [places] + bits(1, 4)), axis=0)
    sums, returned = lax.optimization_barrier((sums, returned))
    parts = group_parts(sums, bits(4, places))
    bias_grad, key_grad, value_grad = closing(parts, key_kept, value_kept, returned)
    return (query_grad[None], key_grad[None], value_grad[None], bias_grad.reshape(-1))


def solution(mesh):
    rows = P("dp", "seq", None)
    return jax.shard_map(
        per_device,
        mesh=mesh,
        in_specs=(rows, rows, rows, rows, rows, P("dp", None)),
        out_specs=(rows, rows, rows, P()),
        check_vma=False,
    )
```

```python
import math

import jax
import jax.numpy as jnp
from jax import lax
from jax.experimental import pallas as pl
from jax.experimental.pallas import tpu as pltpu
from jax.sharding import PartitionSpec as P

HD = 128
ROWS = 128
GROUP = 8
NEG = -1e30
SCALE = 1.0 / math.sqrt(HD)
SCALE2 = SCALE * math.log2(math.e)
NT = (((1,), (1,)), ((), ()))
NN = (((1,), (0,)), ((), ()))
TN = (((0,), (0,)), ((), ()))


VMEM = pl.BlockSpec(memory_space=pltpu.VMEM)
SMEM = pl.BlockSpec(memory_space=pltpu.SMEM)
HBM = pl.BlockSpec(memory_space=pltpu.HBM)


def dot(a, b, dims=NN):
    return lax.dot_general(a, b, dims, preferred_element_type=jnp.float32)


def column(row):
    key = lax.broadcasted_iota(jnp.int32, (ROWS, ROWS), 0)
    at = lax.broadcasted_iota(jnp.int32, (ROWS, ROWS), 1)
    return jnp.sum(jnp.where(key == at, jnp.broadcast_to(row, (ROWS, ROWS)), 0), axis=1, keepdims=True)


def heads(width=HD):
    return [slice(h * width, (h + 1) * width) for h in range(GROUP)]


def own_kernel(
    me_ref, seg_hbm, q_hbm, o_hbm, do_hbm, k_hbm, v_hbm,
    power_ref, slope_ref, qs_ref, dos_ref, keys_ref, stat_ref, before_mask_ref,
    seg_ref, q_ref, o_ref, do_ref, v_ref, sems,
):
    shared = power_ref.shape[0]
    first = [
        pltpu.make_async_copy(src, dst, sems.at[3 * shared + n])
        for n, (src, dst) in enumerate(((seg_hbm, seg_ref), (k_hbm, keys_ref), (v_hbm, v_ref)))
    ]
    for copy in first:
        copy.start()
    copies = []
    for group in range(shared):
        at = pl.ds(group * GROUP * HD, GROUP * HD)
        copies.append(
            [
                pltpu.make_async_copy(src.at[:, at], dst.at[:, at], sems.at[3 * group + n])
                for n, (src, dst) in enumerate(((q_hbm, q_ref), (do_hbm, do_ref), (o_hbm, o_ref)))
            ]
        )
        for copy in copies[-1]:
            copy.start()
    for copy in first:
        copy.wait()
    me = me_ref[0]
    seg = seg_ref[pl.ds(me, 1), :]
    seg_before = seg_ref[pl.ds(jnp.maximum(me - 1, 0), 1), :]
    key = lax.broadcasted_iota(jnp.int32, (ROWS, ROWS), 0)
    row = lax.broadcasted_iota(jnp.int32, (ROWS, ROWS), 1)
    mask = jnp.where((column(seg) == seg) & (key <= row), 0.0, NEG)
    before_mask_ref[...] = jnp.where((column(seg_before) == seg) & (me > 0), 0.0, NEG)
    for group in range(shared):
        for copy in copies[group]:
            copy.wait()
        cols = [slice((group * GROUP + h) * HD, (group * GROUP + h + 1) * HD) for h in range(GROUP)]
        q_all = jnp.concatenate([q_ref[:, c] for c in cols], axis=0)
        do_all = jnp.concatenate([do_ref[:, c] for c in cols], axis=0)
        qs_ref[group] = q_all
        dos_ref[group] = do_all
        mine = slice(group * HD, (group + 1) * HD)
        scores_all = dot(keys_ref[:, mine], q_all, NT)
        grads_all = dot(v_ref[:, mine], do_all, NT)
        for c, at in zip(cols, heads()):
            products = do_ref[:, c].astype(jnp.float32) * o_ref[:, c].astype(jnp.float32)
            delta = jnp.sum(products.T, axis=0, keepdims=True)
            scores = scores_all[:, at] * SCALE2 + mask
            peak = jnp.max(scores, axis=0, keepdims=True)
            powers = jnp.exp2(scores - peak)
            power_ref[group, :, at] = powers
            slope_ref[group, :, at] = powers * (grads_all[:, at] - delta)
            stat_ref[group, 0:1, at] = peak
            stat_ref[group, 1:2, at] = jnp.sum(powers, axis=0, keepdims=True)
            stat_ref[group, 2:3, at] = delta


def weight_kernel(
    power_ref, slope_ref, qs_ref, dos_ref, stat_ref, mask_ref, k_before_ref,
    weight_ref, ds_own_ref, kept_ref, back_ref, sums_ref,
    w_ref,
):
    shared = power_ref.shape[0]
    mask = mask_ref[...]
    def scores_of(group):
        return dot(k_before_ref[:, group * HD : (group + 1) * HD], qs_ref[group], NT)

    ahead = scores_of(0)
    for group in range(shared):
        mine = slice(group * HD, (group + 1) * HD)
        scores_all = ahead
        if group + 1 < shared:
            ahead = scores_of(group + 1)
        for at in heads():
            peak_own = stat_ref[group, 0:1, at]
            scores = scores_all[:, at] * SCALE2 + mask
            peak = jnp.maximum(jnp.max(scores, axis=0, keepdims=True), peak_own)
            powers = jnp.exp2(scores - peak)
            fade = jnp.exp2(peak_own - peak)
            total = jnp.sum(powers, axis=0, keepdims=True) + stat_ref[group, 1:2, at] * fade
            share = 1.0 / total
            weights = powers * share
            share_own = fade * share
            weight_ref[group, :, at] = weights
            w_ref[group, 0:ROWS, at] = weights.astype(jnp.bfloat16)
            w_ref[group, ROWS:, at] = (power_ref[group, :, at] * share_own).astype(jnp.bfloat16)
            ds_own_ref[group, :, at] = (slope_ref[group, :, at] * share_own).astype(jnp.bfloat16)
        value_part = dot(w_ref[group], dos_ref[group])
        back_ref[:, mine] = value_part[:ROWS].astype(jnp.bfloat16)
        kept_ref[:, mine] = value_part[ROWS:]
        sums_ref[group : group + 1, :] = jnp.sum(value_part, axis=0, keepdims=True)


def score_kernel(
    weight_ref, ds_own_ref, qs_ref, dos_ref, stat_ref, keys_ref, k_before_ref, v_before_ref, value_back_ref, value_sums_ref,
    dq_ref, kept_ref, back_ref, copies_ref,
    ds_ref, dq_buf, sums_ref, sems,
):
    shared = weight_ref.shape[0]
    base = shared * GROUP
    back_ref[1] = value_back_ref[...]
    sums_ref[base + shared : base + 2 * shared, :] = value_sums_ref[0:shared, :]
    copies = []

    def grads_of(group):
        return dot(v_before_ref[:, group * HD : (group + 1) * HD], dos_ref[group], NT)

    ahead = grads_of(0)
    for group in range(shared):
        mine = slice(group * HD, (group + 1) * HD)
        keys = jnp.concatenate([k_before_ref[:, mine], keys_ref[:, mine]], axis=0)
        grads_all = ahead
        if group + 1 < shared:
            ahead = grads_of(group + 1)
        ds_ref[group, ROWS:, :] = ds_own_ref[group]
        for at in heads():
            slope = weight_ref[group, :, at] * (grads_all[:, at] - stat_ref[group, 2:3, at])
            ds_ref[group, 0:ROWS, at] = slope.astype(jnp.bfloat16)
        dq_t = (dot(keys.T, ds_ref[group]) * SCALE).astype(jnp.bfloat16)
        for head, at in enumerate(heads()):
            dq = dq_t[:, at].T
            dq_buf[group, :, at] = dq
            row = group * GROUP + head
            sums_ref[row : row + 1, :] = jnp.sum(dq.astype(jnp.float32), axis=0, keepdims=True)
        copies.append(
            pltpu.make_async_copy(
                dq_buf.at[group], dq_ref.at[:, pl.ds(group * GROUP * HD, GROUP * HD)], sems.at[group]
            )
        )
        copies[-1].start()
        key_part = dot(ds_ref[group], qs_ref[group]) * SCALE
        back_ref[0, :, mine] = key_part[:ROWS].astype(jnp.bfloat16)
        kept_ref[:, mine] = key_part[ROWS:]
        sums_ref[base + group : base + group + 1, :] = jnp.sum(key_part, axis=0, keepdims=True)
    for n in range(copies_ref.shape[0]):
        copies.append(pltpu.make_async_copy(sums_ref, copies_ref.at[n], sems.at[shared + n]))
        copies[-1].start()
    for copy in copies:
        copy.wait()


def own_part(me, segments, queries, forward_out, out_grad, keys, values):
    shared = keys.shape[1] // HD
    hbm = [pltpu.with_memory_space_constraint(x, pltpu.HBM) for x in (segments, queries, forward_out, out_grad, keys, values)]
    terms = (shared, ROWS, GROUP * ROWS)
    stacked = (shared, GROUP * ROWS, HD)
    return pl.pallas_call(
        own_kernel,
        in_specs=[SMEM] + [HBM] * 6,
        out_specs=[VMEM] * 7,
        out_shape=[
            pltpu.VMEM(terms, jnp.float32),
            pltpu.VMEM(terms, jnp.float32),
            pltpu.VMEM(stacked, jnp.bfloat16),
            pltpu.VMEM(stacked, jnp.bfloat16),
            pltpu.VMEM(keys.shape, jnp.bfloat16),
            pltpu.VMEM((shared, 8, GROUP * ROWS), jnp.float32),
            pltpu.VMEM((ROWS, ROWS), jnp.float32),
        ],
        scratch_shapes=[
            pltpu.VMEM(segments.shape, jnp.int32),
            pltpu.VMEM(queries.shape, jnp.bfloat16),
            pltpu.VMEM(queries.shape, jnp.bfloat16),
            pltpu.VMEM(queries.shape, jnp.bfloat16),
            pltpu.VMEM(values.shape, jnp.bfloat16),
            pltpu.SemaphoreType.DMA((3 * shared + 3,)),
        ],
        compiler_params=pltpu.CompilerParams(vmem_limit_bytes=32 * 1024 * 1024),
        cost_estimate=pl.CostEstimate(
            flops=4 * 2 * ROWS * ROWS * HD * shared * GROUP,
            bytes_accessed=4 * 1024 * 1024,
            transcendentals=ROWS * ROWS * shared * GROUP,
        ),
    )(me, *hbm)


def pin(*arrays):
    return [pltpu.with_memory_space_constraint(x, pltpu.VMEM) for x in arrays]


def weight_part(terms, keys_before):
    power, slope, queries, grads, _, stats, mask = terms
    shared = power.shape[0]
    return pl.pallas_call(
        weight_kernel,
        in_specs=[VMEM] * 7,
        out_specs=[VMEM] * 5,
        out_shape=[
            pltpu.VMEM(power.shape, jnp.float32),
            pltpu.VMEM(power.shape, jnp.bfloat16),
            pltpu.VMEM(keys_before.shape, jnp.float32),
            pltpu.VMEM(keys_before.shape, jnp.bfloat16),
            pltpu.VMEM((8, HD), jnp.float32),
        ],
        scratch_shapes=[pltpu.VMEM((shared, 2 * ROWS, GROUP * ROWS), jnp.bfloat16)],
        compiler_params=pltpu.CompilerParams(vmem_limit_bytes=24 * 1024 * 1024),
        cost_estimate=pl.CostEstimate(
            flops=3 * 2 * ROWS * ROWS * HD * shared * GROUP,
            bytes_accessed=1024 * 1024,
            transcendentals=ROWS * ROWS * shared * GROUP,
        ),
    )(*pin(power, slope, queries, grads, stats, mask, keys_before))


def score_part(terms, weights, ds_own, keys_before, values_before, value_back, value_sums, peers):
    _, _, queries, grads, keys, stats, _ = terms
    shared = weights.shape[0]
    rows = shared * GROUP + 2 * shared
    return pl.pallas_call(
        score_kernel,
        in_specs=[VMEM] * 10,
        out_specs=[HBM, VMEM, VMEM, HBM],
        out_shape=[
            jax.ShapeDtypeStruct((ROWS, shared * GROUP * HD), jnp.bfloat16),
            pltpu.VMEM(keys.shape, jnp.float32),
            pltpu.VMEM((2,) + keys.shape, jnp.bfloat16),
            jax.ShapeDtypeStruct((peers, rows, HD), jnp.float32),
        ],
        scratch_shapes=[
            pltpu.VMEM((shared, 2 * ROWS, GROUP * ROWS), jnp.bfloat16),
            pltpu.VMEM((shared, ROWS, GROUP * HD), jnp.bfloat16),
            pltpu.VMEM((rows, HD), jnp.float32),
            pltpu.SemaphoreType.DMA((shared + peers,)),
        ],
        compiler_params=pltpu.CompilerParams(vmem_limit_bytes=24 * 1024 * 1024),
        cost_estimate=pl.CostEstimate(
            flops=5 * 2 * ROWS * ROWS * HD * shared * GROUP,
            bytes_accessed=2 * 1024 * 1024,
            transcendentals=0,
        ),
    )(*pin(weights, ds_own, queries, grads, stats, keys, keys_before, values_before, value_back, value_sums))


def exchange(copies, masks):
    span = [0]
    for m in masks:
        span = span + [a ^ m for a in span]
    groups, seen = [], set()
    for i in range(lax.axis_size("seq") * lax.axis_size("dp")):
        if i not in seen:
            groups.append(sorted(i ^ a for a in span))
            seen |= set(groups[-1])
    return lax.all_to_all(
        copies, ("seq", "dp"), split_axis=0, concat_axis=0, tiled=True, axis_index_groups=groups
    )


def group_parts(x, masks):
    return exchange(jnp.broadcast_to(x[None], (1 << len(masks),) + x.shape), masks)


def bits(low, high):
    return [low << i for i in range((high // low).bit_length() - 1)]


def closing_kernel(parts_ref, key_kept_ref, value_kept_ref, returned_ref, bias_ref, key_ref, value_ref):
    bias_ref[...] = jnp.sum(parts_ref[...], axis=0)
    key_ref[...] = (key_kept_ref[...] + returned_ref[0].astype(jnp.float32)).astype(jnp.bfloat16)
    value_ref[...] = (value_kept_ref[...] + returned_ref[1].astype(jnp.float32)).astype(jnp.bfloat16)


def closing(parts, key_kept, value_kept, returned):
    grad = jax.ShapeDtypeStruct(key_kept.shape, jnp.bfloat16)
    return pl.pallas_call(
        closing_kernel,
        in_specs=[VMEM] * 4,
        out_specs=[VMEM] * 3,
        out_shape=[jax.ShapeDtypeStruct(parts.shape[1:], jnp.float32), grad, grad],
    )(*pin(parts, key_kept, value_kept, returned))


def per_device(queries, key_vectors, value_vectors, forward_out, out_grad, segment_number):
    ways = lax.axis_size("seq")
    me = lax.axis_index("seq").astype(jnp.int32).reshape(1)
    onward = [(i, i + 1) for i in range(ways - 1)]
    keys_before = lax.ppermute(key_vectors[0], "seq", onward)
    values_before = lax.ppermute(value_vectors[0], "seq", onward)
    segments = segment_number.reshape(ways, ROWS)
    terms = own_part(
        me, segments, queries[0], forward_out[0], out_grad[0], key_vectors[0], value_vectors[0]
    )
    weights, ds_own, value_kept, value_back, value_sums = weight_part(terms, keys_before)
    query_grad, key_kept, back, copies = score_part(
        terms, weights, ds_own, keys_before, values_before, value_back, value_sums, ways // 2
    )
    returned = lax.ppermute(back, "seq", [(i + 1, i) for i in range(ways - 1)])
    places = lax.axis_size("dp")
    sums = jnp.sum(exchange(copies, bits(2 * places, ways * places)), axis=0)
    sums = jnp.sum(group_parts(sums, [places] + bits(1, 4)), axis=0)
    sums, returned = lax.optimization_barrier((sums, returned))
    parts = group_parts(sums, bits(4, places))
    bias_grad, key_grad, value_grad = closing(parts, key_kept, value_kept, returned)
    return (query_grad[None], key_grad[None], value_grad[None], bias_grad.reshape(-1))


def solution(mesh):
    rows = P("dp", "seq", None)
    return jax.shard_map(
        per_device,
        mesh=mesh,
        in_specs=(rows, rows, rows, rows, rows, P("dp", None)),
        out_specs=(rows, rows, rows, P()),
        check_vma=False,
    )
```

```python
import math

import jax
import jax.numpy as jnp
from jax import lax
from jax.experimental import pallas as pl
from jax.experimental.pallas import tpu as pltpu
from jax.sharding import PartitionSpec as P

HD = 128
ROWS = 128
GROUP = 8
NEG = -1e30
SCALE = 1.0 / math.sqrt(HD)
SCALE2 = SCALE * math.log2(math.e)
NT = (((1,), (1,)), ((), ()))
NN = (((1,), (0,)), ((), ()))
TN = (((0,), (0,)), ((), ()))


VMEM = pl.BlockSpec(memory_space=pltpu.VMEM)
SMEM = pl.BlockSpec(memory_space=pltpu.SMEM)
HBM = pl.BlockSpec(memory_space=pltpu.HBM)


def dot(a, b, dims=NN):
    return lax.dot_general(a, b, dims, preferred_element_type=jnp.float32)


def column(row):
    key = lax.broadcasted_iota(jnp.int32, (ROWS, ROWS), 0)
    at = lax.broadcasted_iota(jnp.int32, (ROWS, ROWS), 1)
    return jnp.sum(jnp.where(key == at, jnp.broadcast_to(row, (ROWS, ROWS)), 0), axis=1, keepdims=True)


def heads(width=HD):
    return [slice(h * width, (h + 1) * width) for h in range(GROUP)]


def own_kernel(
    me_ref, seg_hbm, q_hbm, o_hbm, do_hbm, k_hbm, v_hbm,
    power_ref, slope_ref, qs_ref, dos_ref, keys_ref, stat_ref, before_mask_ref,
    seg_ref, q_ref, o_ref, do_ref, v_ref, sems,
):
    shared = power_ref.shape[0]
    first = [
        pltpu.make_async_copy(src, dst, sems.at[3 * shared + n])
        for n, (src, dst) in enumerate(((seg_hbm, seg_ref), (k_hbm, keys_ref), (v_hbm, v_ref)))
    ]
    for copy in first:
        copy.start()
    copies = []
    for group in range(shared):
        at = pl.ds(group * GROUP * HD, GROUP * HD)
        copies.append(
            [
                pltpu.make_async_copy(src.at[:, at], dst.at[:, at], sems.at[3 * group + n])
                for n, (src, dst) in enumerate(((q_hbm, q_ref), (do_hbm, do_ref), (o_hbm, o_ref)))
            ]
        )
        for copy in copies[-1]:
            copy.start()
    for copy in first:
        copy.wait()
    me = me_ref[0]
    seg = seg_ref[pl.ds(me, 1), :]
    seg_before = seg_ref[pl.ds(jnp.maximum(me - 1, 0), 1), :]
    key = lax.broadcasted_iota(jnp.int32, (ROWS, ROWS), 0)
    row = lax.broadcasted_iota(jnp.int32, (ROWS, ROWS), 1)
    mask = jnp.where((column(seg) == seg) & (key <= row), 0.0, NEG)
    before_mask_ref[...] = jnp.where((column(seg_before) == seg) & (me > 0), 0.0, NEG)
    for group in range(shared):
        for copy in copies[group]:
            copy.wait()
        cols = [slice((group * GROUP + h) * HD, (group * GROUP + h + 1) * HD) for h in range(GROUP)]
        q_all = jnp.concatenate([q_ref[:, c] for c in cols], axis=0)
        do_all = jnp.concatenate([do_ref[:, c] for c in cols], axis=0)
        qs_ref[group] = q_all
        dos_ref[group] = do_all
        mine = slice(group * HD, (group + 1) * HD)
        scores_all = dot(keys_ref[:, mine], q_all, NT)
        grads_all = dot(v_ref[:, mine], do_all, NT)
        for c, at in zip(cols, heads()):
            products = do_ref[:, c].astype(jnp.float32) * o_ref[:, c].astype(jnp.float32)
            delta = jnp.sum(products.T, axis=0, keepdims=True)
            scores = scores_all[:, at] * SCALE2 + mask
            peak = jnp.max(scores, axis=0, keepdims=True)
            powers = jnp.exp2(scores - peak)
            power_ref[group, :, at] = powers
            slope_ref[group, :, at] = powers * (grads_all[:, at] - delta)
            stat_ref[group, 0:1, at] = peak
            stat_ref[group, 1:2, at] = jnp.sum(powers, axis=0, keepdims=True)
            stat_ref[group, 2:3, at] = delta


def weight_kernel(
    power_ref, slope_ref, qs_ref, dos_ref, stat_ref, mask_ref, k_before_ref,
    weight_ref, ds_own_ref, kept_ref, back_ref, sums_ref,
    w_ref,
):
    shared = power_ref.shape[0]
    mask = mask_ref[...]
    def scores_of(group):
        return dot(k_before_ref[:, group * HD : (group + 1) * HD], qs_ref[group], NT)

    ahead = [scores_of(group) for group in range(shared)]
    for group in range(shared):
        mine = slice(group * HD, (group + 1) * HD)
        scores_all = ahead[group]
        for at in heads():
            peak_own = stat_ref[group, 0:1, at]
            scores = scores_all[:, at] * SCALE2 + mask
            peak = jnp.maximum(jnp.max(scores, axis=0, keepdims=True), peak_own)
            powers = jnp.exp2(scores - peak)
            fade = jnp.exp2(peak_own - peak)
            total = jnp.sum(powers, axis=0, keepdims=True) + stat_ref[group, 1:2, at] * fade
            share = 1.0 / total
            weights = powers * share
            share_own = fade * share
            weight_ref[group, :, at] = weights
            w_ref[group, 0:ROWS, at] = weights.astype(jnp.bfloat16)
            w_ref[group, ROWS:, at] = (power_ref[group, :, at] * share_own).astype(jnp.bfloat16)
            ds_own_ref[group, :, at] = (slope_ref[group, :, at] * share_own).astype(jnp.bfloat16)
        value_part = dot(w_ref[group], dos_ref[group])
        back_ref[:, mine] = value_part[:ROWS].astype(jnp.bfloat16)
        kept_ref[:, mine] = value_part[ROWS:]
        sums_ref[group : group + 1, :] = jnp.sum(value_part, axis=0, keepdims=True)


def score_kernel(
    weight_ref, ds_own_ref, qs_ref, dos_ref, stat_ref, keys_ref, k_before_ref, v_before_ref, value_back_ref, value_sums_ref,
    dq_ref, kept_ref, back_ref, copies_ref,
    ds_ref, dq_buf, sums_ref, stack_ref, sems,
):
    shared = weight_ref.shape[0]
    base = shared * GROUP
    back_ref[1] = value_back_ref[...]
    sums_ref[base + shared : base + 2 * shared, :] = value_sums_ref[0:shared, :]
    copies = []

    def grads_of(group):
        return dot(v_before_ref[:, group * HD : (group + 1) * HD], dos_ref[group], NT)

    ahead = [grads_of(group) for group in range(shared)]
    for group in range(shared):
        mine = slice(group * HD, (group + 1) * HD)
        keys = jnp.concatenate([k_before_ref[:, mine], keys_ref[:, mine]], axis=0)
        grads_all = ahead[group]
        ds_ref[group, ROWS:, :] = ds_own_ref[group]
        for at in heads():
            slope = weight_ref[group, :, at] * (grads_all[:, at] - stat_ref[group, 2:3, at])
            ds_ref[group, 0:ROWS, at] = slope.astype(jnp.bfloat16)
        dq_t = (dot(keys.T, ds_ref[group]) * SCALE).astype(jnp.bfloat16)
        for head, at in enumerate(heads()):
            dq = dq_t[:, at].T
            dq_buf[group, :, at] = dq
            row = group * GROUP + head
            sums_ref[row : row + 1, :] = jnp.sum(dq.astype(jnp.float32), axis=0, keepdims=True)
        copies.append(
            pltpu.make_async_copy(
                dq_buf.at[group], dq_ref.at[:, pl.ds(group * GROUP * HD, GROUP * HD)], sems.at[group]
            )
        )
        copies[-1].start()
        key_part = dot(ds_ref[group], qs_ref[group]) * SCALE
        back_ref[0, :, mine] = key_part[:ROWS].astype(jnp.bfloat16)
        kept_ref[:, mine] = key_part[ROWS:]
        sums_ref[base + group : base + group + 1, :] = jnp.sum(key_part, axis=0, keepdims=True)
    for n in range(copies_ref.shape[0]):
        stack_ref[n] = sums_ref[...]
    copies.append(pltpu.make_async_copy(stack_ref, copies_ref, sems.at[shared]))
    copies[-1].start()
    for copy in copies:
        copy.wait()


def own_part(me, segments, queries, forward_out, out_grad, keys, values):
    shared = keys.shape[1] // HD
    hbm = [pltpu.with_memory_space_constraint(x, pltpu.HBM) for x in (segments, queries, forward_out, out_grad, keys, values)]
    terms = (shared, ROWS, GROUP * ROWS)
    stacked = (shared, GROUP * ROWS, HD)
    return pl.pallas_call(
        own_kernel,
        in_specs=[SMEM] + [HBM] * 6,
        out_specs=[VMEM] * 7,
        out_shape=[
            pltpu.VMEM(terms, jnp.float32),
            pltpu.VMEM(terms, jnp.float32),
            pltpu.VMEM(stacked, jnp.bfloat16),
            pltpu.VMEM(stacked, jnp.bfloat16),
            pltpu.VMEM(keys.shape, jnp.bfloat16),
            pltpu.VMEM((shared, 8, GROUP * ROWS), jnp.float32),
            pltpu.VMEM((ROWS, ROWS), jnp.float32),
        ],
        scratch_shapes=[
            pltpu.VMEM(segments.shape, jnp.int32),
            pltpu.VMEM(queries.shape, jnp.bfloat16),
            pltpu.VMEM(queries.shape, jnp.bfloat16),
            pltpu.VMEM(queries.shape, jnp.bfloat16),
            pltpu.VMEM(values.shape, jnp.bfloat16),
            pltpu.SemaphoreType.DMA((3 * shared + 3,)),
        ],
        compiler_params=pltpu.CompilerParams(vmem_limit_bytes=32 * 1024 * 1024),
        cost_estimate=pl.CostEstimate(
            flops=4 * 2 * ROWS * ROWS * HD * shared * GROUP,
            bytes_accessed=4 * 1024 * 1024,
            transcendentals=ROWS * ROWS * shared * GROUP,
        ),
    )(me, *hbm)


def pin(*arrays):
    return [pltpu.with_memory_space_constraint(x, pltpu.VMEM) for x in arrays]


def weight_part(terms, keys_before):
    power, slope, queries, grads, _, stats, mask = terms
    shared = power.shape[0]
    return pl.pallas_call(
        weight_kernel,
        in_specs=[VMEM] * 7,
        out_specs=[VMEM] * 5,
        out_shape=[
            pltpu.VMEM(power.shape, jnp.float32),
            pltpu.VMEM(power.shape, jnp.bfloat16),
            pltpu.VMEM(keys_before.shape, jnp.float32),
            pltpu.VMEM(keys_before.shape, jnp.bfloat16),
            pltpu.VMEM((8, HD), jnp.float32),
        ],
        scratch_shapes=[pltpu.VMEM((shared, 2 * ROWS, GROUP * ROWS), jnp.bfloat16)],
        compiler_params=pltpu.CompilerParams(vmem_limit_bytes=24 * 1024 * 1024),
        cost_estimate=pl.CostEstimate(
            flops=3 * 2 * ROWS * ROWS * HD * shared * GROUP,
            bytes_accessed=1024 * 1024,
            transcendentals=ROWS * ROWS * shared * GROUP,
        ),
    )(*pin(power, slope, queries, grads, stats, mask, keys_before))


def score_part(terms, weights, ds_own, keys_before, values_before, value_back, value_sums, peers):
    _, _, queries, grads, keys, stats, _ = terms
    shared = weights.shape[0]
    rows = shared * GROUP + 2 * shared
    return pl.pallas_call(
        score_kernel,
        in_specs=[VMEM] * 10,
        out_specs=[HBM, VMEM, VMEM, HBM],
        out_shape=[
            jax.ShapeDtypeStruct((ROWS, shared * GROUP * HD), jnp.bfloat16),
            pltpu.VMEM(keys.shape, jnp.float32),
            pltpu.VMEM((2,) + keys.shape, jnp.bfloat16),
            jax.ShapeDtypeStruct((peers, rows, HD), jnp.float32),
        ],
        scratch_shapes=[
            pltpu.VMEM((shared, 2 * ROWS, GROUP * ROWS), jnp.bfloat16),
            pltpu.VMEM((shared, ROWS, GROUP * HD), jnp.bfloat16),
            pltpu.VMEM((rows, HD), jnp.float32),
            pltpu.VMEM((peers, rows, HD), jnp.float32),
            pltpu.SemaphoreType.DMA((shared + 1,)),
        ],
        compiler_params=pltpu.CompilerParams(vmem_limit_bytes=24 * 1024 * 1024),
        cost_estimate=pl.CostEstimate(
            flops=5 * 2 * ROWS * ROWS * HD * shared * GROUP,
            bytes_accessed=2 * 1024 * 1024,
            transcendentals=0,
        ),
    )(*pin(weights, ds_own, queries, grads, stats, keys, keys_before, values_before, value_back, value_sums))


def exchange(copies, masks):
    span = [0]
    for m in masks:
        span = span + [a ^ m for a in span]
    groups, seen = [], set()
    for i in range(lax.axis_size("seq") * lax.axis_size("dp")):
        if i not in seen:
            groups.append(sorted(i ^ a for a in span))
            seen |= set(groups[-1])
    return lax.all_to_all(
        copies, ("seq", "dp"), split_axis=0, concat_axis=0, tiled=True, axis_index_groups=groups
    )


def group_parts(x, masks):
    return exchange(jnp.broadcast_to(x[None], (1 << len(masks),) + x.shape), masks)


def bits(low, high):
    return [low << i for i in range((high // low).bit_length() - 1)]


def closing_kernel(parts_ref, key_kept_ref, value_kept_ref, returned_ref, bias_ref, key_ref, value_ref):
    bias_ref[...] = jnp.sum(parts_ref[...], axis=0)
    key_ref[...] = (key_kept_ref[...] + returned_ref[0].astype(jnp.float32)).astype(jnp.bfloat16)
    value_ref[...] = (value_kept_ref[...] + returned_ref[1].astype(jnp.float32)).astype(jnp.bfloat16)


def closing(parts, key_kept, value_kept, returned):
    grad = jax.ShapeDtypeStruct(key_kept.shape, jnp.bfloat16)
    return pl.pallas_call(
        closing_kernel,
        in_specs=[VMEM] * 4,
        out_specs=[VMEM] * 3,
        out_shape=[jax.ShapeDtypeStruct(parts.shape[1:], jnp.float32), grad, grad],
    )(*pin(parts, key_kept, value_kept, returned))


def per_device(queries, key_vectors, value_vectors, forward_out, out_grad, segment_number):
    ways = lax.axis_size("seq")
    me = lax.axis_index("seq").astype(jnp.int32).reshape(1)
    onward = [(i, i + 1) for i in range(ways - 1)]
    keys_before = lax.ppermute(key_vectors[0], "seq", onward)
    values_before = lax.ppermute(value_vectors[0], "seq", onward)
    segments = segment_number.reshape(ways, ROWS)
    terms = own_part(
        me, segments, queries[0], forward_out[0], out_grad[0], key_vectors[0], value_vectors[0]
    )
    weights, ds_own, value_kept, value_back, value_sums = weight_part(terms, keys_before)
    query_grad, key_kept, back, copies = score_part(
        terms, weights, ds_own, keys_before, values_before, value_back, value_sums, lax.axis_size("dp") // 4
    )
    returned = lax.ppermute(back, "seq", [(i + 1, i) for i in range(ways - 1)])
    places = lax.axis_size("dp")
    sums = jnp.sum(exchange(copies, bits(4, places)), axis=0)
    sums = jnp.sum(group_parts(sums, [places] + bits(1, 4)), axis=0)
    sums, returned = lax.optimization_barrier((sums, returned))
    parts = group_parts(sums, bits(2 * places, ways * places))
    bias_grad, key_grad, value_grad = closing(parts, key_kept, value_kept, returned)
    return (query_grad[None], key_grad[None], value_grad[None], bias_grad.reshape(-1))


def solution(mesh):
    rows = P("dp", "seq", None)
    return jax.shard_map(
        per_device,
        mesh=mesh,
        in_specs=(rows, rows, rows, rows, rows, P("dp", None)),
        out_specs=(rows, rows, rows, P()),
        check_vma=False,
    )
```

```python
import math

import jax
import jax.numpy as jnp
from jax import lax
from jax.experimental import pallas as pl
from jax.experimental.pallas import tpu as pltpu
from jax.sharding import PartitionSpec as P

HD = 128
ROWS = 128
GROUP = 8
NEG = -1e30
SCALE = 1.0 / math.sqrt(HD)
SCALE2 = SCALE * math.log2(math.e)
NT = (((1,), (1,)), ((), ()))
NN = (((1,), (0,)), ((), ()))
TN = (((0,), (0,)), ((), ()))


VMEM = pl.BlockSpec(memory_space=pltpu.VMEM)
SMEM = pl.BlockSpec(memory_space=pltpu.SMEM)
HBM = pl.BlockSpec(memory_space=pltpu.HBM)


def dot(a, b, dims=NN):
    return lax.dot_general(a, b, dims, preferred_element_type=jnp.float32)


def column(row):
    key = lax.broadcasted_iota(jnp.int32, (ROWS, ROWS), 0)
    at = lax.broadcasted_iota(jnp.int32, (ROWS, ROWS), 1)
    return jnp.sum(jnp.where(key == at, jnp.broadcast_to(row, (ROWS, ROWS)), 0), axis=1, keepdims=True)


def heads(width=HD):
    return [slice(h * width, (h + 1) * width) for h in range(GROUP)]


def own_kernel(
    me_ref, seg_hbm, q_hbm, o_hbm, do_hbm, k_hbm, v_hbm,
    power_ref, slope_ref, qs_ref, dos_ref, keys_ref, stat_ref, before_mask_ref,
    seg_ref, q_ref, o_ref, do_ref, v_ref, sems,
):
    shared = power_ref.shape[0]
    first = [
        pltpu.make_async_copy(src, dst, sems.at[3 * shared + n])
        for n, (src, dst) in enumerate(((seg_hbm, seg_ref), (k_hbm, keys_ref), (v_hbm, v_ref)))
    ]
    for copy in first:
        copy.start()
    copies = []
    for group in range(shared):
        at = pl.ds(group * GROUP * HD, GROUP * HD)
        copies.append(
            [
                pltpu.make_async_copy(src.at[:, at], dst.at[:, at], sems.at[3 * group + n])
                for n, (src, dst) in enumerate(((q_hbm, q_ref), (do_hbm, do_ref), (o_hbm, o_ref)))
            ]
        )
        for copy in copies[-1]:
            copy.start()
    for copy in first:
        copy.wait()
    me = me_ref[0]
    seg = seg_ref[pl.ds(me, 1), :]
    seg_before = seg_ref[pl.ds(jnp.maximum(me - 1, 0), 1), :]
    key = lax.broadcasted_iota(jnp.int32, (ROWS, ROWS), 0)
    row = lax.broadcasted_iota(jnp.int32, (ROWS, ROWS), 1)
    mask = jnp.where((column(seg) == seg) & (key <= row), 0.0, NEG)
    before_mask_ref[...] = jnp.where((column(seg_before) == seg) & (me > 0), 0.0, NEG)
    for group in range(shared):
        for copy in copies[group]:
            copy.wait()
        cols = [slice((group * GROUP + h) * HD, (group * GROUP + h + 1) * HD) for h in range(GROUP)]
        q_all = jnp.concatenate([q_ref[:, c] for c in cols], axis=0)
        do_all = jnp.concatenate([do_ref[:, c] for c in cols], axis=0)
        qs_ref[group] = q_all
        dos_ref[group] = do_all
        mine = slice(group * HD, (group + 1) * HD)
        scores_all = dot(keys_ref[:, mine], q_all, NT)
        grads_all = dot(v_ref[:, mine], do_all, NT)
        for c, at in zip(cols, heads()):
            products = do_ref[:, c].astype(jnp.float32) * o_ref[:, c].astype(jnp.float32)
            delta = jnp.sum(products.T, axis=0, keepdims=True)
            scores = scores_all[:, at] * SCALE2 + mask
            peak = jnp.max(scores, axis=0, keepdims=True)
            powers = jnp.exp2(scores - peak)
            power_ref[group, :, at] = powers
            slope_ref[group, :, at] = powers * (grads_all[:, at] - delta)
            stat_ref[group, 0:1, at] = peak
            stat_ref[group, 1:2, at] = jnp.sum(powers, axis=0, keepdims=True)
            stat_ref[group, 2:3, at] = delta


def weight_kernel(
    power_ref, slope_ref, qs_ref, dos_ref, stat_ref, mask_ref, k_before_ref,
    weight_ref, ds_own_ref, kept_ref, back_ref, sums_ref,
    w_ref,
):
    shared = power_ref.shape[0]
    mask = mask_ref[...]
    def scores_of(group):
        return dot(k_before_ref[:, group * HD : (group + 1) * HD], qs_ref[group], NT)

    ahead = [scores_of(group) for group in range(shared)]
    for group in range(shared):
        mine = slice(group * HD, (group + 1) * HD)
        scores_all = ahead[group]
        for at in heads():
            peak_own = stat_ref[group, 0:1, at]
            scores = scores_all[:, at] * SCALE2 + mask
            peak = jnp.maximum(jnp.max(scores, axis=0, keepdims=True), peak_own)
            powers = jnp.exp2(scores - peak)
            fade = jnp.exp2(peak_own - peak)
            total = jnp.sum(powers, axis=0, keepdims=True) + stat_ref[group, 1:2, at] * fade
            share = 1.0 / total
            weights = powers * share
            share_own = fade * share
            weight_ref[group, :, at] = weights
            w_ref[group, 0:ROWS, at] = weights.astype(jnp.bfloat16)
            w_ref[group, ROWS:, at] = (power_ref[group, :, at] * share_own).astype(jnp.bfloat16)
            ds_own_ref[group, :, at] = (slope_ref[group, :, at] * share_own).astype(jnp.bfloat16)
        value_part = dot(w_ref[group], dos_ref[group])
        back_ref[:, mine] = value_part[:ROWS].astype(jnp.bfloat16)
        kept_ref[:, mine] = value_part[ROWS:]
        sums_ref[group : group + 1, :] = jnp.sum(value_part, axis=0, keepdims=True)


def score_kernel(
    weight_ref, ds_own_ref, qs_ref, dos_ref, stat_ref, keys_ref, k_before_ref, v_before_ref, value_back_ref, value_sums_ref,
    dq_ref, kept_ref, back_ref, copies_ref,
    ds_ref, dq_buf, sums_ref, stack_ref, sems,
):
    shared = weight_ref.shape[0]
    base = shared * GROUP
    back_ref[1] = value_back_ref[...]
    sums_ref[base + shared : base + 2 * shared, :] = value_sums_ref[0:shared, :]
    copies = []

    def grads_of(group):
        return dot(v_before_ref[:, group * HD : (group + 1) * HD], dos_ref[group], NT)

    ahead = [grads_of(group) for group in range(shared)]
    for group in range(shared):
        mine = slice(group * HD, (group + 1) * HD)
        keys = jnp.concatenate([k_before_ref[:, mine], keys_ref[:, mine]], axis=0)
        grads_all = ahead[group]
        ds_ref[group, ROWS:, :] = ds_own_ref[group]
        for at in heads():
            slope = weight_ref[group, :, at] * (grads_all[:, at] - stat_ref[group, 2:3, at])
            ds_ref[group, 0:ROWS, at] = slope.astype(jnp.bfloat16)
        dq_t = (dot(keys.T, ds_ref[group]) * SCALE).astype(jnp.bfloat16)
        for head, at in enumerate(heads()):
            dq = dq_t[:, at].T
            dq_buf[group, :, at] = dq
            row = group * GROUP + head
            sums_ref[row : row + 1, :] = jnp.sum(dq.astype(jnp.float32), axis=0, keepdims=True)
        copies.append(
            pltpu.make_async_copy(
                dq_buf.at[group], dq_ref.at[:, pl.ds(group * GROUP * HD, GROUP * HD)], sems.at[group]
            )
        )
        copies[-1].start()
        key_part = dot(ds_ref[group], qs_ref[group]) * SCALE
        back_ref[0, :, mine] = key_part[:ROWS].astype(jnp.bfloat16)
        kept_ref[:, mine] = key_part[ROWS:]
        sums_ref[base + group : base + group + 1, :] = jnp.sum(key_part, axis=0, keepdims=True)
    for n in range(copies_ref.shape[0]):
        stack_ref[n] = sums_ref[...]
    copies.append(pltpu.make_async_copy(stack_ref, copies_ref, sems.at[shared]))
    copies[-1].start()
    for copy in copies:
        copy.wait()


def own_part(me, segments, queries, forward_out, out_grad, keys, values):
    shared = keys.shape[1] // HD
    hbm = [pltpu.with_memory_space_constraint(x, pltpu.HBM) for x in (segments, queries, forward_out, out_grad, keys, values)]
    terms = (shared, ROWS, GROUP * ROWS)
    stacked = (shared, GROUP * ROWS, HD)
    return pl.pallas_call(
        own_kernel,
        in_specs=[SMEM] + [HBM] * 6,
        out_specs=[VMEM] * 7,
        out_shape=[
            pltpu.VMEM(terms, jnp.float32),
            pltpu.VMEM(terms, jnp.float32),
            pltpu.VMEM(stacked, jnp.bfloat16),
            pltpu.VMEM(stacked, jnp.bfloat16),
            pltpu.VMEM(keys.shape, jnp.bfloat16),
            pltpu.VMEM((shared, 8, GROUP * ROWS), jnp.float32),
            pltpu.VMEM((ROWS, ROWS), jnp.float32),
        ],
        scratch_shapes=[
            pltpu.VMEM(segments.shape, jnp.int32),
            pltpu.VMEM(queries.shape, jnp.bfloat16),
            pltpu.VMEM(queries.shape, jnp.bfloat16),
            pltpu.VMEM(queries.shape, jnp.bfloat16),
            pltpu.VMEM(values.shape, jnp.bfloat16),
            pltpu.SemaphoreType.DMA((3 * shared + 3,)),
        ],
        compiler_params=pltpu.CompilerParams(vmem_limit_bytes=32 * 1024 * 1024),
        cost_estimate=pl.CostEstimate(
            flops=4 * 2 * ROWS * ROWS * HD * shared * GROUP,
            bytes_accessed=4 * 1024 * 1024,
            transcendentals=ROWS * ROWS * shared * GROUP,
        ),
    )(me, *hbm)


def pin(*arrays):
    return [pltpu.with_memory_space_constraint(x, pltpu.VMEM) for x in arrays]


def weight_part(terms, keys_before):
    power, slope, queries, grads, _, stats, mask = terms
    shared = power.shape[0]
    return pl.pallas_call(
        weight_kernel,
        in_specs=[VMEM] * 7,
        out_specs=[VMEM] * 5,
        out_shape=[
            pltpu.VMEM(power.shape, jnp.float32),
            pltpu.VMEM(power.shape, jnp.bfloat16),
            pltpu.VMEM(keys_before.shape, jnp.float32),
            pltpu.VMEM(keys_before.shape, jnp.bfloat16),
            pltpu.VMEM((8, HD), jnp.float32),
        ],
        scratch_shapes=[pltpu.VMEM((shared, 2 * ROWS, GROUP * ROWS), jnp.bfloat16)],
        compiler_params=pltpu.CompilerParams(vmem_limit_bytes=24 * 1024 * 1024),
        cost_estimate=pl.CostEstimate(
            flops=3 * 2 * ROWS * ROWS * HD * shared * GROUP,
            bytes_accessed=1024 * 1024,
            transcendentals=ROWS * ROWS * shared * GROUP,
        ),
    )(*pin(power, slope, queries, grads, stats, mask, keys_before))


def score_part(terms, weights, ds_own, keys_before, values_before, value_back, value_sums, peers):
    _, _, queries, grads, keys, stats, _ = terms
    shared = weights.shape[0]
    rows = shared * GROUP + 2 * shared
    return pl.pallas_call(
        score_kernel,
        in_specs=[VMEM] * 10,
        out_specs=[HBM, VMEM, VMEM, HBM],
        out_shape=[
            jax.ShapeDtypeStruct((ROWS, shared * GROUP * HD), jnp.bfloat16),
            pltpu.VMEM(keys.shape, jnp.float32),
            pltpu.VMEM((2,) + keys.shape, jnp.bfloat16),
            jax.ShapeDtypeStruct((peers, rows, HD), jnp.float32),
        ],
        scratch_shapes=[
            pltpu.VMEM((shared, 2 * ROWS, GROUP * ROWS), jnp.bfloat16),
            pltpu.VMEM((shared, ROWS, GROUP * HD), jnp.bfloat16),
            pltpu.VMEM((rows, HD), jnp.float32),
            pltpu.VMEM((peers, rows, HD), jnp.float32),
            pltpu.SemaphoreType.DMA((shared + 1,)),
        ],
        compiler_params=pltpu.CompilerParams(vmem_limit_bytes=24 * 1024 * 1024),
        cost_estimate=pl.CostEstimate(
            flops=5 * 2 * ROWS * ROWS * HD * shared * GROUP,
            bytes_accessed=2 * 1024 * 1024,
            transcendentals=0,
        ),
    )(*pin(weights, ds_own, queries, grads, stats, keys, keys_before, values_before, value_back, value_sums))


def exchange(copies, masks):
    span = [0]
    for m in masks:
        span = span + [a ^ m for a in span]
    groups, seen = [], set()
    for i in range(lax.axis_size("seq") * lax.axis_size("dp")):
        if i not in seen:
            groups.append(sorted(i ^ a for a in span))
            seen |= set(groups[-1])
    return lax.all_to_all(
        copies, ("seq", "dp"), split_axis=0, concat_axis=0, tiled=True, axis_index_groups=groups
    )


def group_parts(x, masks):
    return exchange(jnp.broadcast_to(x[None], (1 << len(masks),) + x.shape), masks)


def bits(low, high):
    return [low << i for i in range((high // low).bit_length() - 1)]


def closing_kernel(parts_ref, key_kept_ref, value_kept_ref, returned_ref, bias_ref, key_ref, value_ref):
    bias_ref[...] = jnp.sum(parts_ref[...], axis=0)
    key_ref[...] = (key_kept_ref[...] + returned_ref[0].astype(jnp.float32)).astype(jnp.bfloat16)
    value_ref[...] = (value_kept_ref[...] + returned_ref[1].astype(jnp.float32)).astype(jnp.bfloat16)


def closing(parts, key_kept, value_kept, returned):
    grad = jax.ShapeDtypeStruct(key_kept.shape, jnp.bfloat16)
    return pl.pallas_call(
        closing_kernel,
        in_specs=[VMEM] * 4,
        out_specs=[VMEM] * 3,
        out_shape=[jax.ShapeDtypeStruct(parts.shape[1:], jnp.float32), grad, grad],
    )(*pin(parts, key_kept, value_kept, returned))


def per_device(queries, key_vectors, value_vectors, forward_out, out_grad, segment_number):
    ways = lax.axis_size("seq")
    me = lax.axis_index("seq").astype(jnp.int32).reshape(1)
    onward = [(i, i + 1) for i in range(ways - 1)]
    keys_before = lax.ppermute(key_vectors[0], "seq", onward)
    values_before = lax.ppermute(value_vectors[0], "seq", onward)
    segments = segment_number.reshape(ways, ROWS)
    terms = own_part(
        me, segments, queries[0], forward_out[0], out_grad[0], key_vectors[0], value_vectors[0]
    )
    weights, ds_own, value_kept, value_back, value_sums = weight_part(terms, keys_before)
    query_grad, key_kept, back, copies = score_part(
        terms, weights, ds_own, keys_before, values_before, value_back, value_sums, ways // 2
    )
    returned = lax.ppermute(back, "seq", [(i + 1, i) for i in range(ways - 1)])
    places = lax.axis_size("dp")
    sums = jnp.sum(exchange(copies, bits(2 * places, ways * places)), axis=0)
    sums = jnp.sum(group_parts(sums, [places] + bits(1, 4)), axis=0)
    sums, returned = lax.optimization_barrier((sums, returned))
    parts = group_parts(sums, bits(4, places))
    bias_grad, key_grad, value_grad = closing(parts, key_kept, value_kept, returned)
    return (query_grad[None], key_grad[None], value_grad[None], bias_grad.reshape(-1))


def solution(mesh):
    rows = P("dp", "seq", None)
    return jax.shard_map(
        per_device,
        mesh=mesh,
        in_specs=(rows, rows, rows, rows, rows, P("dp", None)),
        out_specs=(rows, rows, rows, P()),
        check_vma=False,
    )
```
